128 devices in a mesh: seq: 8 (over y, z_hi), fsdp: 16 (over z_lo, x, core).
Axes of the slice: x: 4, y: 4, z: 4 (z_hi: 2, z_lo: 2; z = z_hi * 2 + z_lo), core: 2. Of those that a mesh axis runs over, the one named last changes fastest.
Arguments:
- hidden_in: bfloat16 [16, 1024, 5120], P('fsdp', 'seq'), may hold values from -6 to 6
- queries: bfloat16 [16, 1024, 4096], P('fsdp', 'seq'), may hold values from -48 to 48
- saved_keys: bfloat16 [16, 1024, 512], P('fsdp', 'seq'), may hold values from -6 to 6
- value_matrix: bfloat16 [5120, 512], P('fsdp'), may hold values from -0.078125 to 0.078125
- output_gradient: bfloat16 [16, 1024, 4096], P('fsdp', 'seq'), may hold values from -6 to 6
- passage_index: int32 [16, 1024], P('fsdp'), may hold values from 0 to 11, never falling along the last dimension, each value on 1 to 169 neighbouring positions
Outputs:
- query_gradients: bfloat16 [16, 1024, 4096], P('fsdp', 'seq')
- key_gradients: bfloat16 [16, 1024, 512], P('fsdp', 'seq')
- grad_input: bfloat16 [16, 1024, 5120], P('fsdp', 'seq')
- grad_weight: float32 [5120, 512], P('fsdp')
The draws below stay inside these ranges and needn't reach their ends.
Inputs may be any that keep to these rules, and one draw needn't show every extreme that they name: `passage_index`: never falls along a list; passage 0 is the list's header, which every later token of the list sees; each passage has 1 to 169 tokens.
All inputs are finite; a program needn't handle non-finite values.
Results may differ from the reference program's by a relative error of at most 0.007.
Values may be sent and summed in bfloat16 or wider, within the bound.
No kernel may reach another device: no remote copies, remote signals or barrier semaphores. Data moves between devices by JAX's collectives and lax.ppermute only.
A program may use at most 128 MiB of HBM per device.

```python
import math
import jax
import jax.numpy as jnp
import numpy as np
from jax import lax

MODEL_WIDTH = 5120
QUERY_HEADS = 32
KEY_HEADS = 4
HEAD_WIDTH = 128
LIST_LENGTH = 1024
PASSAGES = 12
PMOST = 169
LIST_BATCH = 16


def shared_keys(key):
    gaussian_key = jax.random.fold_in(key, 0)
    gaussian_draws = jax.random.normal(gaussian_key, (LIST_BATCH, LIST_LENGTH, KEY_HEADS, HEAD_WIDTH), jnp.float32)
    return gaussian_draws


def draw_saved_keys(key, part):
    gaussian_draws = shared_keys(key)
    table_entries = jnp.clip(gaussian_draws, -6.0, 6.0)
    return table_entries.reshape(LIST_BATCH, LIST_LENGTH, KEY_HEADS * HEAD_WIDTH).astype(jnp.bfloat16)


def draw_queries(key, part):
    key = jax.random.fold_in(key, 5)
    base_key = jax.random.fold_in(key, 0)
    table_entries = jnp.clip(jax.random.normal(base_key, (LIST_BATCH, LIST_LENGTH, QUERY_HEADS, HEAD_WIDTH), jnp.float32), -6.0, 6.0)
    return table_entries.reshape(LIST_BATCH, LIST_LENGTH, QUERY_HEADS * HEAD_WIDTH).astype(jnp.bfloat16)


def raised(drawn, rng, source, target, shards_of, factor):
    def block_of(dim):
        return (jnp.arange(drawn.shape[dim]) // (drawn.shape[dim] // shards_of)).reshape((-1,) + (1,) * (drawn.ndim - 1 - dim))

    one_side = jax.random.permutation(rng, shards_of)[block_of(target)]
    other_side = (block_of(target) + shards_of // 2) % shards_of
    return jnp.where((block_of(source) == one_side) | (block_of(source) == other_side), factor * drawn, drawn)


def steps_of(own_key, dims, pieces, low, high):
    loudness, own = 1.0, jax.random.fold_in(own_key, 6)
    for dim, blocks in pieces:
        draws = jnp.exp(jax.random.uniform(jax.random.fold_in(own, dim), (blocks,), jnp.float32, low / len(pieces), high / len(pieces)))
        loudness = loudness * jnp.repeat(draws, dims[dim] // blocks).reshape([-1 if axis == dim else 1 for axis in range(len(dims))])
    return loudness


def split_up(amount, total, most, slope):
    weights = [(1 << 20) // math.isqrt(rank ** slope) + 1 for rank in range(2, amount + 1)]
    spare, counts = total - most - (amount - 1), [1] * (amount - 1)
    while spare > 0:
        movable = [i for i in range(amount - 1) if counts[i] < most]
        pool, left = sum([weights[i] for i in movable]), spare
        for i in movable:
            addition = min(most - counts[i], max(1, left * weights[i] // pool), spare)
            counts[i] = counts[i] + addition
            spare = spare - addition
    return np.array([most] + counts)


def ragged_sizes(stream_key, number_of, total, reach, skew):
    if number_of == 2:
        one = jax.random.randint(stream_key, (), max(1, total - reach), min(reach, total - 1) + 1)
        return jnp.stack([one, total - one])
    sizes = jnp.asarray(split_up(number_of, total, reach, skew), jnp.int32)
    pairs = (number_of - 1) // 2
    source_of, taker = sizes[1:1 + 2 * pairs:2], sizes[2:2 + 2 * pairs:2]
    room = jnp.minimum(source_of - 1, reach - taker)
    passed = jax.random.randint(jax.random.fold_in(stream_key, 1), (pairs,), 0, 1 << 20) % (room + 1)
    sizes = sizes.at[1:1 + 2 * pairs:2].set(source_of - passed).at[2:2 + 2 * pairs:2].set(taker + passed)
    return sizes[jax.random.permutation(jax.random.fold_in(stream_key, 2), number_of)]


def normal_values(stream_key, dims, spread, limit, pieces=(), dtype=jnp.bfloat16):
    level = steps_of(stream_key, dims, pieces, -0.22, 0.18) if pieces else 1.0
    values = jax.random.normal(stream_key, dims, jnp.float32) * spread * level
    return jnp.minimum(jnp.maximum(values, -limit), limit).astype(dtype)


def gaussian_with(stream_key, shape, width, bound, cuts, heavy, held_as=jnp.bfloat16):
    array = width * jax.random.normal(stream_key, shape, jnp.float32)
    if cuts:
        array = array * steps_of(stream_key, shape, cuts, -0.22, 0.18)
    return jnp.clip(raised(array, jax.random.fold_in(stream_key, 3), *heavy), -bound, bound).astype(held_as)


def setup_inputs(seed: int = 0) -> dict:
    streams_of = jax.random.split(jax.random.key(seed), 7)
    return {
        "hidden_in": gaussian_with(streams_of[0], (LIST_BATCH, LIST_LENGTH, MODEL_WIDTH), 1.0, 6.0, ((0, 16), (1, 8)), (1, 2, 8, 2.0)),
        "queries": draw_queries(jax.random.fold_in(streams_of[6], 71), 0),
        "saved_keys": draw_saved_keys(jax.random.fold_in(streams_of[6], 71), 0),
        "value_matrix": normal_values(streams_of[3], (MODEL_WIDTH, KEY_HEADS * HEAD_WIDTH), MODEL_WIDTH ** -0.5, 0.078125, ((0, 16),)),
        "output_gradient": normal_values(streams_of[4], (LIST_BATCH, LIST_LENGTH, QUERY_HEADS * HEAD_WIDTH), 1.0, 6.0, ((0, 16), (1, 8))),
        "passage_index": jax.vmap(lambda own: jnp.searchsorted(jnp.cumsum(ragged_sizes(own, PASSAGES, LIST_LENGTH, PMOST, 1)), jnp.arange(LIST_LENGTH), side="right"))(jax.random.split(streams_of[5], LIST_BATCH)).reshape((LIST_BATCH, LIST_LENGTH)).astype(jnp.int32),
    }


def attend(members):
    q_group, k_group, v_group, grad_group, segments = members
    inv_root = 1.0 / math.sqrt(HEAD_WIDTH)
    position = jnp.arange(LIST_LENGTH)
    allowed = (position[None, :] <= position[:, None]) & ((segments[None, :] == segments[:, None]) | (segments[None, :] == 0))
    q_float = q_group.astype(jnp.float32)
    k_float = k_group.astype(jnp.float32)
    v_float = v_group.astype(jnp.float32)
    g_float = grad_group.astype(jnp.float32)
    scores = jnp.einsum('igd,jd->gij', q_float, k_float) * inv_root
    scores = jnp.where(allowed[None], scores, -jnp.inf)
    highest = lax.optimization_barrier(jnp.max(scores, axis=-1, keepdims=True))
    weights = jnp.exp(scores - highest)
    prob_full = weights / lax.optimization_barrier(jnp.sum(weights, axis=-1, keepdims=True))
    dprobs = jnp.einsum('igd,jd->gij', g_float, v_float)
    row_delta = lax.optimization_barrier(jnp.sum(prob_full * dprobs, axis=-1, keepdims=True))
    dscores = lax.optimization_barrier((prob_full * (dprobs - row_delta) * inv_root).astype(jnp.bfloat16))
    probs_half = lax.optimization_barrier(prob_full.astype(jnp.bfloat16))
    dscores_f = dscores.astype(jnp.float32)
    probs_f = probs_half.astype(jnp.float32)
    query_gradient = jnp.einsum('gij,jd->igd', dscores_f, k_float).astype(jnp.bfloat16)
    key_gradient_sum = jnp.einsum('gij,igd->jd', dscores_f, q_float)
    value_gradient_sum = jnp.einsum('gij,igd->jd', probs_f, g_float)
    return (query_gradient, key_gradient_sum.astype(jnp.bfloat16), value_gradient_sum.astype(jnp.bfloat16))

def reference(hidden_in, queries, saved_keys, value_matrix, output_gradient, passage_index):
    head_groups = QUERY_HEADS // KEY_HEADS
    flat_input = hidden_in.reshape(LIST_BATCH * LIST_LENGTH, MODEL_WIDTH)
    value_rows_all = jnp.dot(flat_input, value_matrix, preferred_element_type=jnp.float32).astype(jnp.bfloat16)
    query_items = queries.reshape(LIST_BATCH, LIST_LENGTH, KEY_HEADS, head_groups, HEAD_WIDTH).transpose(0, 2, 1, 3, 4).reshape(LIST_BATCH * KEY_HEADS, LIST_LENGTH, head_groups, HEAD_WIDTH)
    key_items = saved_keys.reshape(LIST_BATCH, LIST_LENGTH, KEY_HEADS, HEAD_WIDTH).transpose(0, 2, 1, 3).reshape(LIST_BATCH * KEY_HEADS, LIST_LENGTH, HEAD_WIDTH)
    value_items = value_rows_all.reshape(LIST_BATCH, LIST_LENGTH, KEY_HEADS, HEAD_WIDTH).transpose(0, 2, 1, 3).reshape(LIST_BATCH * KEY_HEADS, LIST_LENGTH, HEAD_WIDTH)
    gradient_items = output_gradient.reshape(LIST_BATCH, LIST_LENGTH, KEY_HEADS, head_groups, HEAD_WIDTH).transpose(0, 2, 1, 3, 4).reshape(LIST_BATCH * KEY_HEADS, LIST_LENGTH, head_groups, HEAD_WIDTH)
    segment_items = jnp.repeat(passage_index, KEY_HEADS, axis=0)
    query_gradient, key_gradient, value_gradient = lax.map(attend, (query_items, key_items, value_items, gradient_items, segment_items))
    query_gradients = query_gradient.reshape(LIST_BATCH, KEY_HEADS, LIST_LENGTH, head_groups, HEAD_WIDTH).transpose(0, 2, 1, 3, 4).reshape(LIST_BATCH, LIST_LENGTH, QUERY_HEADS * HEAD_WIDTH)
    key_gradients = key_gradient.reshape(LIST_BATCH, KEY_HEADS, LIST_LENGTH, HEAD_WIDTH).transpose(0, 2, 1, 3).reshape(LIST_BATCH, LIST_LENGTH, KEY_HEADS * HEAD_WIDTH)
    value_weight_gradient = value_gradient.reshape(LIST_BATCH, KEY_HEADS, LIST_LENGTH, HEAD_WIDTH).transpose(0, 2, 1, 3).reshape(LIST_BATCH * LIST_LENGTH, KEY_HEADS * HEAD_WIDTH)
    grad_input = jnp.dot(value_weight_gradient, value_matrix.T, preferred_element_type=jnp.float32).astype(jnp.bfloat16).reshape(LIST_BATCH, LIST_LENGTH, MODEL_WIDTH)
    grad_weight = jnp.dot(flat_input.T, value_weight_gradient, preferred_element_type=jnp.float32)
    return (query_gradients, key_gradients, grad_input, grad_weight)
```

```python
import math

import jax
import jax.numpy as jnp
from jax import lax
from jax.experimental import pallas as pl
from jax.experimental.pallas import tpu as pltpu
from jax.sharding import Mesh
from jax.sharding import PartitionSpec as P

KEY_HEADS = 4
GROUP = 8
HEAD = 128
ROWS = 128
BACK = 192
SLOTS = 2 * BACK + ROWS
SEQ = ("y", "zh")
FSDP = ("zl", "x", "c")
SWAP = ((0, 1), (1, 0))
ROOT = 1.0 / math.sqrt(HEAD)
BF = jnp.bfloat16
F32 = jnp.float32


def stacked(ref):
    return jnp.concatenate([ref[:, h * HEAD : (h + 1) * HEAD] for h in range(GROUP)], axis=0)


def probs_kernel(q_ref, k_ref, g_ref, bias_ref, p_ref, dv_ref):
    scores = lax.dot_general(
        k_ref[...], stacked(q_ref), (((1,), (1,)), ((), ())), preferred_element_type=F32
    )
    bias = bias_ref[...]
    scores = scores + jnp.concatenate([bias] * GROUP, axis=1)
    highest = jnp.max(scores, axis=0, keepdims=True)
    weights = jnp.exp((scores - highest) * ROOT)
    total = jnp.sum(weights, axis=0, keepdims=True)
    probs = (weights * (1.0 / total)).astype(BF)
    p_ref[0] = probs
    dv_ref[...] = jnp.dot(probs, stacked(g_ref), preferred_element_type=F32)


def scores_kernel(q_ref, k_ref, g_ref, v_ref, p_ref, dq_ref, dk_ref):
    dprobs = lax.dot_general(
        v_ref[...], stacked(g_ref), (((1,), (1,)), ((), ())), preferred_element_type=F32
    )
    probs = p_ref[0].astype(F32)
    delta = jnp.sum(probs * dprobs, axis=0, keepdims=True)
    dscores = (probs * (dprobs - delta) * ROOT).astype(BF)
    dk_ref[...] = jnp.dot(dscores, stacked(q_ref), preferred_element_type=F32)
    dq = lax.dot_general(
        k_ref[...], dscores, (((0,), (0,)), ((), ())), preferred_element_type=F32
    )
    for h in range(GROUP):
        part = slice(h * HEAD, (h + 1) * HEAD)
        dq_ref[:, part] = dq[:, part].T.astype(BF)


def column(rows, width):
    return pl.BlockSpec((rows, width), lambda g: (0, g))


def probs_call(q, k, g, bias):
    return pl.pallas_call(
        probs_kernel,
        grid=(KEY_HEADS,),
        in_specs=[
            column(ROWS, GROUP * HEAD),
            column(SLOTS, HEAD),
            column(ROWS, GROUP * HEAD),
            pl.BlockSpec((SLOTS, ROWS), lambda g: (0, 0)),
        ],
        out_specs=[
            pl.BlockSpec((1, SLOTS, GROUP * ROWS), lambda g: (g, 0, 0)),
            column(SLOTS, HEAD),
        ],
        out_shape=[
            jax.ShapeDtypeStruct((KEY_HEADS, SLOTS, GROUP * ROWS), BF),
            jax.ShapeDtypeStruct((SLOTS, KEY_HEADS * HEAD), F32),
        ],
        compiler_params=pltpu.CompilerParams(vmem_limit_bytes=40 << 20),
        cost_estimate=pl.CostEstimate(
            flops=4 * SLOTS * ROWS * 32 * HEAD, bytes_accessed=8 << 20, transcendentals=SLOTS * ROWS * 32
        ),
        name="probs",
    )(q, k, g, bias)


def scores_call(q, k, g, v, p):
    return pl.pallas_call(
        scores_kernel,
        grid=(KEY_HEADS,),
        in_specs=[
            column(ROWS, GROUP * HEAD),
            column(SLOTS, HEAD),
            column(ROWS, GROUP * HEAD),
            column(SLOTS, HEAD),
            pl.BlockSpec((1, SLOTS, GROUP * ROWS), lambda g: (g, 0, 0)),
        ],
        out_specs=[column(ROWS, GROUP * HEAD), column(SLOTS, HEAD)],
        out_shape=[
            jax.ShapeDtypeStruct((ROWS, KEY_HEADS * GROUP * HEAD), BF),
            jax.ShapeDtypeStruct((SLOTS, KEY_HEADS * HEAD), F32),
        ],
        compiler_params=pltpu.CompilerParams(vmem_limit_bytes=40 << 20),
        cost_estimate=pl.CostEstimate(
            flops=6 * SLOTS * ROWS * 32 * HEAD, bytes_accessed=8 << 20, transcendentals=0
        ),
        name="scores",
    )(q, k, g, v, p)


def spread(block, y, zh):
    other = lax.ppermute(block, "zh", SWAP)
    pair = jnp.where(
        zh == 0, jnp.concatenate([block, other]), jnp.concatenate([other, block])
    )
    before = lax.ppermute(pair, "y", ((0, 1), (1, 2), (2, 3)))
    to_last = lax.ppermute(pair[:BACK], "y", ((0, 3),))
    to_third = lax.ppermute(pair[:BACK], "y", ((0, 2),))
    header = jnp.where(
        y == 0,
        pair[:BACK],
        jnp.where(y == 1, before[:BACK], jnp.where(y == 2, to_third, to_last)),
    )
    window = jnp.where(
        zh == 0, before[2 * ROWS - BACK :], jnp.concatenate([before[BACK:], other])
    )
    return jnp.concatenate([header, window, block])


def collected(slots, y, zh):
    header, window, own = slots[:BACK], slots[BACK : 2 * BACK], slots[2 * BACK :]
    tail = 2 * ROWS - BACK
    zeros = jnp.zeros((2 * ROWS, slots.shape[1]), F32)
    before = jnp.where(
        zh == 0,
        zeros.at[tail:].set(window),
        zeros.at[BACK:].set(window[:tail]),
    ) + jnp.where(y == 1, zeros.at[:BACK].set(header), 0.0)
    half_header = header.astype(BF)
    from_next = lax.ppermute(before.astype(BF), "y", ((1, 0), (2, 1), (3, 2)))
    from_last = lax.ppermute(half_header, "y", ((3, 0),))
    from_third = lax.ppermute(half_header, "y", ((2, 0),))
    first = header + from_last.astype(F32) + from_third.astype(F32)
    pair = from_next.astype(F32) + jnp.where(y == 0, zeros.at[:BACK].set(first), 0.0)
    low, high = pair[:ROWS], pair[ROWS:]
    low = low + jnp.where(zh == 1, window[tail:], 0.0)
    sent = lax.ppermute(jnp.where(zh == 0, high, low).astype(BF), "zh", SWAP)
    return own + jnp.where(zh == 0, low, high) + sent.astype(F32)


def slot_bias(passages, s):
    token = s * ROWS + jnp.arange(ROWS)
    mine = lax.dynamic_slice(passages, (s * ROWS,), (ROWS,))
    padded = jnp.concatenate([jnp.zeros((BACK,), passages.dtype), passages])
    near = lax.dynamic_slice(padded, (s * ROWS,), (BACK + ROWS,))
    head_ok = (passages[:BACK, None] == 0) & (jnp.arange(BACK)[:, None] <= token[None])
    near_token = s * ROWS - BACK + jnp.arange(BACK + ROWS)
    near_ok = (
        (near[:, None] == mine[None])
        & (near[:, None] != 0)
        & (near_token[:, None] <= token[None])
    )
    return jnp.where(jnp.concatenate([head_ok, near_ok]), 0.0, -1e30).astype(F32)


def on_device(hidden_in, queries, saved_keys, value_matrix, output_gradient, passage_index):
    y, zh, c = lax.axis_index("y"), lax.axis_index("zh"), lax.axis_index("c")
    s = lax.axis_index(SEQ)
    hidden, q, k, g = hidden_in[0], queries[0], saved_keys[0], output_gradient[0]
    width = hidden.shape[1]
    kv = k.shape[1]
    each = width // 16
    weight = lax.all_gather(value_matrix, FSDP, axis=0, tiled=True)
    by_x = hidden.reshape(ROWS, 2, 4, 2, each).transpose(2, 0, 1, 3, 4).reshape(4, ROWS, 4 * each)
    crossed = lax.all_to_all(by_x, "x", 0, 0)
    bias = slot_bias(passage_index[0], s)
    k_slots = spread(k, y, zh)
    probs, dv_slots = probs_call(q, k_slots, g, bias)
    value_grad = collected(dv_slots, y, zh).astype(BF)
    gathered = lax.all_to_all(jnp.broadcast_to(value_grad[None], (4, ROWS, kv)), "x", 0, 0)
    term = lax.dot_general(
        crossed.reshape(4 * ROWS, 4 * each),
        gathered.reshape(4 * ROWS, kv),
        (((0,), (0,)), ((), ())),
        preferred_element_type=F32,
    ).reshape(2, 2, each, kv)
    kept = lax.dynamic_index_in_dim(term, c, 1, keepdims=False)
    given = lax.dynamic_index_in_dim(term, 1 - c, 1, keepdims=False).astype(BF)
    term = kept + lax.ppermute(given, "c", SWAP).astype(F32)
    pieces = term.astype(BF).reshape(2, 8, each // 8, kv).transpose(1, 0, 2, 3)
    pieces = lax.all_to_all(
        pieces.reshape(16, each // 8, kv), ("y", "zh", "zl"), 0, 0
    )
    piece = jnp.sum(pieces.astype(F32), axis=0).astype(BF)
    grad_weight = lax.all_to_all(
        jnp.broadcast_to(piece[None], (8,) + piece.shape), SEQ, 0, 0
    )
    grad_weight = grad_weight.reshape(each, kv).astype(F32)

    values = jnp.dot(hidden, weight, preferred_element_type=F32).astype(BF)
    v_slots = spread(values, y, zh)
    dq, dk_slots = scores_call(q, k_slots, g, v_slots, probs)
    key_grad = collected(dk_slots, y, zh).astype(BF)
    grad_input = lax.dot_general(
        value_grad, weight, (((1,), (1,)), ((), ())), preferred_element_type=F32
    ).astype(BF)
    return dq[None], key_grad[None], grad_input[None], grad_weight


def solution(mesh):
    fine = Mesh(mesh.devices.reshape(4, 2, 2, 4, 2), ("y", "zh", "zl", "x", "c"))
    tokens = P(FSDP, SEQ, None)
    return jax.shard_map(
        on_device,
        mesh=fine,
        in_specs=(tokens, tokens, tokens, P(FSDP, None), tokens, P(FSDP, None)),
        out_specs=(tokens, tokens, tokens, P(FSDP, None)),
        check_vma=False,
    )
```

```python
import math

import jax
import jax.numpy as jnp
from jax import lax
from jax.experimental import pallas as pl
from jax.experimental.pallas import tpu as pltpu
from jax.sharding import Mesh
from jax.sharding import PartitionSpec as P

KEY_HEADS = 4
GROUP = 8
HEAD = 128
ROWS = 128
BACK = 192
SLOTS = 2 * BACK + ROWS
SEQ = ("y", "zh")
FSDP = ("zl", "x", "c")
SWAP = ((0, 1), (1, 0))
ROOT = 1.0 / math.sqrt(HEAD)
BF = jnp.bfloat16
F32 = jnp.float32


def stacked(ref):
    return jnp.concatenate([ref[:, h * HEAD : (h + 1) * HEAD] for h in range(GROUP)], axis=0)


def probs_kernel(q_ref, k_ref, g_ref, bias_ref, p_ref, dv_ref):
    scores = lax.dot_general(
        k_ref[...], stacked(q_ref), (((1,), (1,)), ((), ())), preferred_element_type=F32
    )
    bias = bias_ref[...]
    scores = scores + jnp.concatenate([bias] * GROUP, axis=1)
    highest = jnp.max(scores, axis=0, keepdims=True)
    weights = jnp.exp((scores - highest) * ROOT)
    total = jnp.sum(weights, axis=0, keepdims=True)
    probs = (weights * (1.0 / total)).astype(BF)
    p_ref[0] = probs
    dv_ref[...] = jnp.dot(probs, stacked(g_ref), preferred_element_type=F32)


def scores_kernel(q_ref, k_ref, g_ref, v_ref, p_ref, dq_ref, dk_ref):
    dprobs = lax.dot_general(
        v_ref[...], stacked(g_ref), (((1,), (1,)), ((), ())), preferred_element_type=F32
    )
    probs = p_ref[0].astype(F32)
    delta = jnp.sum(probs * dprobs, axis=0, keepdims=True)
    dscores = (probs * (dprobs - delta) * ROOT).astype(BF)
    dk_ref[...] = jnp.dot(dscores, stacked(q_ref), preferred_element_type=F32)
    dq = lax.dot_general(
        k_ref[...], dscores, (((0,), (0,)), ((), ())), preferred_element_type=F32
    )
    for h in range(GROUP):
        part = slice(h * HEAD, (h + 1) * HEAD)
        dq_ref[:, part] = dq[:, part].T.astype(BF)


def column(rows, width):
    return pl.BlockSpec((rows, width), lambda g: (0, g))


def probs_call(q, k, g, bias):
    return pl.pallas_call(
        probs_kernel,
        grid=(KEY_HEADS,),
        in_specs=[
            column(ROWS, GROUP * HEAD),
            column(SLOTS, HEAD),
            column(ROWS, GROUP * HEAD),
            pl.BlockSpec((SLOTS, ROWS), lambda g: (0, 0)),
        ],
        out_specs=[
            pl.BlockSpec((1, SLOTS, GROUP * ROWS), lambda g: (g, 0, 0)),
            column(SLOTS, HEAD),
        ],
        out_shape=[
            jax.ShapeDtypeStruct((KEY_HEADS, SLOTS, GROUP * ROWS), BF),
            jax.ShapeDtypeStruct((SLOTS, KEY_HEADS * HEAD), F32),
        ],
        compiler_params=pltpu.CompilerParams(vmem_limit_bytes=24 << 20),
        cost_estimate=pl.CostEstimate(
            flops=4 * SLOTS * ROWS * 32 * HEAD, bytes_accessed=8 << 20, transcendentals=SLOTS * ROWS * 32
        ),
        name="probs",
    )(q, k, g, bias)


def scores_call(q, k, g, v, p):
    return pl.pallas_call(
        scores_kernel,
        grid=(KEY_HEADS,),
        in_specs=[
            column(ROWS, GROUP * HEAD),
            column(SLOTS, HEAD),
            column(ROWS, GROUP * HEAD),
            column(SLOTS, HEAD),
            pl.BlockSpec((1, SLOTS, GROUP * ROWS), lambda g: (g, 0, 0)),
        ],
        out_specs=[column(ROWS, GROUP * HEAD), column(SLOTS, HEAD)],
        out_shape=[
            jax.ShapeDtypeStruct((ROWS, KEY_HEADS * GROUP * HEAD), BF),
            jax.ShapeDtypeStruct((SLOTS, KEY_HEADS * HEAD), F32),
        ],
        compiler_params=pltpu.CompilerParams(vmem_limit_bytes=24 << 20),
        cost_estimate=pl.CostEstimate(
            flops=6 * SLOTS * ROWS * 32 * HEAD, bytes_accessed=8 << 20, transcendentals=0
        ),
        name="scores",
    )(q, k, g, v, p)


def slot_bias(passages, s):
    token = s * ROWS + jnp.arange(ROWS)
    mine = lax.dynamic_slice(passages, (s * ROWS,), (ROWS,))
    padded = jnp.concatenate([jnp.zeros((BACK,), passages.dtype), passages])
    near = lax.dynamic_slice(padded, (s * ROWS,), (BACK + ROWS,))
    head_ok = (passages[:BACK, None] == 0) & (jnp.arange(BACK)[:, None] <= token[None])
    near_token = s * ROWS - BACK + jnp.arange(BACK + ROWS)
    near_ok = (
        (near[:, None] == mine[None])
        & (near[:, None] != 0)
        & (near_token[:, None] <= token[None])
    )
    return jnp.where(jnp.concatenate([head_ok, near_ok]), 0.0, -1e30).astype(F32)


def turned(count, step):
    return tuple((i, (i + step) % count) for i in range(count))


def block_at(array, index):
    return lax.dynamic_index_in_dim(array, index, 0, keepdims=False)


def after(value, *others):
    return lax.optimization_barrier((value,) + others)[0]


def paired(block, zh):
    other = lax.ppermute(block, "zh", SWAP)
    pair = jnp.where(
        zh == 0, jnp.concatenate([block, other]), jnp.concatenate([other, block])
    )
    return other, pair


def spread(block, other, pair, y, zh):
    before = lax.ppermute(pair, "y", turned(4, 1))
    to_third = lax.ppermute(pair[:BACK], "y", turned(4, 2))
    to_last = lax.ppermute(pair[:BACK], "y", turned(4, 3))
    header = jnp.where(
        y == 0,
        pair[:BACK],
        jnp.where(y == 1, before[:BACK], jnp.where(y == 2, to_third, to_last)),
    )
    window = jnp.where(
        zh == 0, before[2 * ROWS - BACK :], jnp.concatenate([before[BACK:], other])
    )
    return jnp.concatenate([header, window, block])


def parted(slots, y, zh):
    header, window = slots[:BACK], slots[BACK : 2 * BACK]
    tail = 2 * ROWS - BACK
    zeros = jnp.zeros((2 * ROWS, slots.shape[1]), F32)
    before = jnp.where(
        zh == 0,
        zeros.at[tail:].set(window),
        zeros.at[BACK:].set(window[:tail]),
    ) + jnp.where(y == 1, zeros.at[:BACK].set(header), 0.0)
    return before.astype(BF), header.astype(BF)


def collected(slots, before, half_header, y, zh):
    header, window, own = slots[:BACK], slots[BACK : 2 * BACK], slots[2 * BACK :]
    tail = 2 * ROWS - BACK
    zeros = jnp.zeros((2 * ROWS, slots.shape[1]), F32)
    from_next = lax.ppermute(before, "y", turned(4, 3))
    from_last = lax.ppermute(half_header, "y", turned(4, 1))
    from_third = lax.ppermute(half_header, "y", turned(4, 2))
    first = header + from_last.astype(F32) + from_third.astype(F32)
    pair = from_next.astype(F32) + jnp.where(y == 0, zeros.at[:BACK].set(first), 0.0)
    low, high = pair[:ROWS], pair[ROWS:]
    low = low + jnp.where(zh == 1, window[tail:], 0.0)
    sent = lax.ppermute(jnp.where(zh == 0, high, low).astype(BF), "zh", SWAP)
    return own + jnp.where(zh == 0, low, high) + sent.astype(F32)


def on_device(hidden_in, queries, saved_keys, value_matrix, output_gradient, passage_index):
    y, zh, zl = lax.axis_index("y"), lax.axis_index("zh"), lax.axis_index("zl")
    x, c = lax.axis_index("x"), lax.axis_index("c")
    z, s = lax.axis_index(("zh", "zl")), lax.axis_index(SEQ)
    hidden, q, k, g = hidden_in[0], queries[0], saved_keys[0], output_gradient[0]
    width, kv = hidden.shape[1], k.shape[1]
    each, half = width // 16, width // 2
    two = 2 * each

    k_other, k_pair = paired(k, zh)
    k_slots = spread(k, k_other, k_pair, y, zh)

    by_x = jnp.stack(
        [
            jnp.concatenate(
                [hidden[:, i * two : (i + 1) * two], hidden[:, half + i * two : half + (i + 1) * two]],
                axis=1,
            )
            for i in range(4)
        ]
    )
    crossed = lax.all_to_all(by_x, "x", 0, 0).reshape(4 * ROWS, 4 * each)
    across = lax.ppermute(value_matrix, "zl", SWAP)
    planes = jnp.where(
        zl == 0, jnp.stack([value_matrix, across]), jnp.stack([across, value_matrix])
    )
    sibling = lax.ppermute(planes, "c", SWAP)
    weight = jnp.where(
        c == 0, jnp.stack([planes, sibling], 1), jnp.stack([sibling, planes], 1)
    ).reshape(4 * each, kv)

    bias = slot_bias(passage_index[0], s)
    probs, dv_slots = probs_call(q, k_slots, g, bias)
    dv_slots = after(dv_slots, crossed)
    dv_before, dv_header = parted(dv_slots, y, zh)

    part = jnp.dot(
        after(crossed, dv_before, dv_header), weight, preferred_element_type=F32
    ).reshape(4, ROWS, kv)
    values = block_at(part, x)
    for step in (1, 2, 3):
        sent = block_at(part, (x + step) % 4).astype(BF)
        values = values + lax.ppermute(sent, "x", turned(4, step)).astype(F32)
    values = values.astype(BF)
    v_other, v_pair = paired(values, zh)

    value_grad = collected(dv_slots, dv_before, dv_header, y, zh).astype(BF)

    v_slots = spread(values, v_other, after(v_pair, value_grad), y, zh)

    near = [value_grad] + [lax.ppermute(value_grad, "x", turned(4, n)) for n in (1, 2, 3)]
    gathered = jnp.concatenate(
        [
            jnp.where(
                x == i,
                near[0],
                jnp.where(
                    x == (i + 1) % 4, near[1], jnp.where(x == (i + 2) % 4, near[2], near[3])
                ),
            )
            for i in range(4)
        ]
    )
    term = lax.dot_general(
        crossed, gathered, (((0,), (0,)), ((), ())), preferred_element_type=F32
    ).reshape(2, 2, each, kv)
    kept = lax.dynamic_index_in_dim(term, c, 1, keepdims=False)
    given = lax.dynamic_index_in_dim(term, 1 - c, 1, keepdims=False).astype(BF)
    back = lax.dot_general(
        gathered, weight, (((1,), (1,)), ((), ())), preferred_element_type=F32
    ).astype(BF)

    term = kept + lax.ppermute(given, "c", SWAP).astype(F32)
    term = term.reshape(2, 2, each // 2, kv)

    def quarter(at):
        return lax.dynamic_slice(term, (at % 2, at // 2, 0, 0), (1, 1, each // 2, kv))[0, 0]

    own_quarter = quarter(z)
    quarters = [quarter((z + step) % 4).astype(BF) for step in (1, 2, 3)]

    v_slots = after(v_slots, back, *quarters)
    dq, dk_slots = scores_call(q, k_slots, g, v_slots, probs)
    dk_before, dk_header = parted(dk_slots, y, zh)

    total = own_quarter
    for step, sent in zip((1, 2, 3), quarters):
        total = total + lax.ppermute(sent, ("zh", "zl"), turned(4, step)).astype(F32)
    mine = total.astype(BF)
    first, second, third = (lax.ppermute(mine, "y", turned(4, n)).astype(F32) for n in (1, 2, 3))
    total = ((mine.astype(F32) + second) + (first + third)).astype(BF)
    other = lax.ppermute(total, "zh", SWAP)
    grad_weight = jnp.where(
        zh == 0, jnp.concatenate([total, other]), jnp.concatenate([other, total])
    ).astype(F32)

    back = lax.all_to_all(back.reshape(4, ROWS, 4 * each), "x", 0, 0)
    grad_input = jnp.concatenate(
        [back[i][:, p * two : (p + 1) * two] for p in range(2) for i in range(4)], axis=1
    )

    key_grad = collected(dk_slots, dk_before, dk_header, y, zh).astype(BF)
    return dq[None], key_grad[None], grad_input[None], grad_weight


def solution(mesh):
    fine = Mesh(mesh.devices.reshape(4, 2, 2, 4, 2), ("y", "zh", "zl", "x", "c"))
    tokens = P(FSDP, SEQ, None)
    return jax.shard_map(
        on_device,
        mesh=fine,
        in_specs=(tokens, tokens, tokens, P(FSDP, None), tokens, P(FSDP, None)),
        out_specs=(tokens, tokens, tokens, P(FSDP, None)),
        check_vma=False,
    )
```

```python
import math

import jax
import jax.numpy as jnp
from jax import lax
from jax.experimental import pallas as pl
from jax.experimental.pallas import tpu as pltpu
from jax.sharding import Mesh
from jax.sharding import PartitionSpec as P

KEY_HEADS = 4
GROUP = 8
HEAD = 128
ROWS = 128
BACK = 192
SLOTS = 2 * BACK + ROWS
SEQ = ("y", "zh")
FSDP = ("zl", "x", "c")
SWAP = ((0, 1), (1, 0))
ROOT = 1.0 / math.sqrt(HEAD)
BF = jnp.bfloat16
F32 = jnp.float32


def stacked(ref):
    return jnp.concatenate([ref[:, h * HEAD : (h + 1) * HEAD] for h in range(GROUP)], axis=0)


def probs_kernel(q_ref, k_ref, g_ref, bias_ref, p_ref, dv_ref):
    scores = lax.dot_general(
        k_ref[...], stacked(q_ref), (((1,), (1,)), ((), ())), preferred_element_type=F32
    )
    bias = bias_ref[...]
    scores = scores + jnp.concatenate([bias] * GROUP, axis=1)
    highest = jnp.max(scores, axis=0, keepdims=True)
    weights = jnp.exp((scores - highest) * ROOT)
    total = jnp.sum(weights, axis=0, keepdims=True)
    probs = (weights * (1.0 / total)).astype(BF)
    p_ref[0] = probs
    dv_ref[...] = jnp.dot(probs, stacked(g_ref), preferred_element_type=F32)


def scores_kernel(q_ref, k_ref, g_ref, v_ref, p_ref, dq_ref, dk_ref):
    dprobs = lax.dot_general(
        v_ref[...], stacked(g_ref), (((1,), (1,)), ((), ())), preferred_element_type=F32
    )
    probs = p_ref[0].astype(F32)
    delta = jnp.sum(probs * dprobs, axis=0, keepdims=True)
    dscores = (probs * (dprobs - delta) * ROOT).astype(BF)
    dk_ref[...] = jnp.dot(dscores, stacked(q_ref), preferred_element_type=F32)
    dq = lax.dot_general(
        k_ref[...], dscores, (((0,), (0,)), ((), ())), preferred_element_type=F32
    )
    for h in range(GROUP):
        part = slice(h * HEAD, (h + 1) * HEAD)
        dq_ref[:, part] = dq[:, part].T.astype(BF)


def far(value):
    return pltpu.with_memory_space_constraint(value, pltpu.HBM)


def column(rows, width):
    return pl.BlockSpec((rows, width), lambda g: (0, g))


def probs_call(q, k, g, bias):
    return pl.pallas_call(
        probs_kernel,
        grid=(KEY_HEADS,),
        in_specs=[
            column(ROWS, GROUP * HEAD),
            column(SLOTS, HEAD),
            column(ROWS, GROUP * HEAD),
            pl.BlockSpec((SLOTS, ROWS), lambda g: (0, 0)),
        ],
        out_specs=[
            pl.BlockSpec((1, SLOTS, GROUP * ROWS), lambda g: (g, 0, 0)),
            column(SLOTS, HEAD),
        ],
        out_shape=[
            pltpu.HBM((KEY_HEADS, SLOTS, GROUP * ROWS), BF),
            jax.ShapeDtypeStruct((SLOTS, KEY_HEADS * HEAD), F32),
        ],
        compiler_params=pltpu.CompilerParams(vmem_limit_bytes=24 << 20),
        cost_estimate=pl.CostEstimate(
            flops=4 * SLOTS * ROWS * 32 * HEAD, bytes_accessed=8 << 20, transcendentals=SLOTS * ROWS * 32
        ),
        name="probs",
    )(q, k, g, bias)


def scores_call(q, k, g, v, p):
    return pl.pallas_call(
        scores_kernel,
        grid=(KEY_HEADS,),
        in_specs=[
            column(ROWS, GROUP * HEAD),
            column(SLOTS, HEAD),
            column(ROWS, GROUP * HEAD),
            column(SLOTS, HEAD),
            pl.BlockSpec((1, SLOTS, GROUP * ROWS), lambda g: (g, 0, 0)),
        ],
        out_specs=[column(ROWS, GROUP * HEAD), column(SLOTS, HEAD)],
        out_shape=[
            jax.ShapeDtypeStruct((ROWS, KEY_HEADS * GROUP * HEAD), BF),
            jax.ShapeDtypeStruct((SLOTS, KEY_HEADS * HEAD), F32),
        ],
        compiler_params=pltpu.CompilerParams(vmem_limit_bytes=24 << 20),
        cost_estimate=pl.CostEstimate(
            flops=6 * SLOTS * ROWS * 32 * HEAD, bytes_accessed=8 << 20, transcendentals=0
        ),
        name="scores",
    )(far(q), k, far(g), v, far(p))


def slot_bias(passages, s):
    token = s * ROWS + jnp.arange(ROWS)
    mine = lax.dynamic_slice(passages, (s * ROWS,), (ROWS,))
    padded = jnp.concatenate([jnp.zeros((BACK,), passages.dtype), passages])
    near = lax.dynamic_slice(padded, (s * ROWS,), (BACK + ROWS,))
    head_ok = (passages[:BACK, None] == 0) & (jnp.arange(BACK)[:, None] <= token[None])
    near_token = s * ROWS - BACK + jnp.arange(BACK + ROWS)
    near_ok = (
        (near[:, None] == mine[None])
        & (near[:, None] != 0)
        & (near_token[:, None] <= token[None])
    )
    return jnp.where(jnp.concatenate([head_ok, near_ok]), 0.0, -1e30).astype(F32)


def grads_kernel(at_ref, crossed_ref, weight_ref, *refs):
    nears, (back_ref, kept_ref, given_ref, gathered_ref) = refs[:4], refs[4:]
    x, c = at_ref[0], at_ref[1]
    for n in range(4):
        row = pl.multiple_of((x + 4 - n) % 4 * ROWS, ROWS)
        gathered_ref[pl.ds(row, ROWS), :] = nears[n][...]
    gathered = gathered_ref[...]
    term = lax.dot_general(
        crossed_ref[...], gathered, (((0,), (0,)), ((), ())), preferred_element_type=F32
    )
    each = term.shape[0] // 2
    kept_ref[0] = jnp.where(c == 0, term[:each], term[each:])
    given_ref[0] = jnp.where(c == 0, term[each:], term[:each]).astype(BF)
    back_ref[...] = lax.dot_general(
        gathered, weight_ref[...], (((1,), (1,)), ((), ())), preferred_element_type=F32
    ).astype(BF)


def grads_call(at, crossed, weight, nears):
    rows, columns = crossed.shape
    kv, half, each = weight.shape[1], columns // 2, columns // 4
    piece = pl.BlockSpec((1, each, kv), lambda i, at: (i, 0, 0))
    return pl.pallas_call(
        grads_kernel,
        grid_spec=pltpu.PrefetchScalarGridSpec(
            num_scalar_prefetch=1,
            grid=(2,),
            in_specs=[
                pl.BlockSpec((rows, half), lambda i, at: (0, i)),
                pl.BlockSpec((half, kv), lambda i, at: (i, 0)),
            ]
            + [pl.BlockSpec((ROWS, kv), lambda i, at: (0, 0))] * 4,
            out_specs=[pl.BlockSpec((rows, half), lambda i, at: (0, i)), piece, piece],
            scratch_shapes=[pltpu.VMEM((rows, kv), BF)],
        ),
        out_shape=[
            pltpu.HBM((rows, columns), BF),
            pltpu.HBM((2, each, kv), F32),
            jax.ShapeDtypeStruct((2, each, kv), BF),
        ],
        compiler_params=pltpu.CompilerParams(vmem_limit_bytes=24 << 20),
        cost_estimate=pl.CostEstimate(
            flops=4 * rows * columns * kv, bytes_accessed=8 << 20, transcendentals=0
        ),
        name="grads",
    )(at, crossed, weight, *nears)


def turned(count, step):
    return tuple((i, (i + step) % count) for i in range(count))


def block_at(array, index):
    return lax.dynamic_index_in_dim(array, index, 0, keepdims=False)


def after(value, *others):
    return lax.optimization_barrier((value,) + others)[0]


def held(values, others):
    return lax.optimization_barrier((tuple(values), tuple(others)))[0]


def turns(value, axis, count, steps=(1, 2, 3)):
    return [lax.ppermute(value, axis, turned(count, n)) for n in steps]


def nearby(block, y, zh):
    before, third, last = turns(block, "y", 4)
    header = jnp.where(
        y == 0, block, jnp.where(y == 1, before, jnp.where(y == 2, third, last))
    )
    return before, header, jnp.concatenate([jnp.where(zh == 0, block, before), header])


def placed(block, before, header, other, zh):
    tail = 2 * ROWS - BACK
    nearest, header_too = other[:ROWS], other[ROWS:]
    low = jnp.where(zh == 0, header, header_too)
    high = jnp.where(zh == 0, header_too, header)
    return jnp.concatenate([low, high[:tail], before[tail:], nearest, block])


def parted(slots, zh):
    low = slots[:ROWS]
    high = jnp.concatenate([slots[ROWS:BACK], jnp.zeros_like(slots[BACK:2 * ROWS])])
    nearest = slots[2 * BACK - ROWS : 2 * BACK]
    sent = jnp.concatenate([nearest, jnp.where(zh == 0, high, low)]).astype(BF)
    return jnp.where(zh == 0, low, high), sent


def joined(slots, header, other, y, zh):
    nearest, header_too = other[:ROWS].astype(F32), other[ROWS:].astype(F32)
    header = header + header_too
    tail = slots[BACK : 2 * BACK - ROWS]
    before = jnp.concatenate([jnp.zeros_like(tail), tail])
    before = before + jnp.where(zh == 1, nearest, 0.0) + jnp.where(y == 1, header, 0.0)
    own = slots[2 * BACK :] + jnp.where(zh == 0, nearest, 0.0) + jnp.where(y == 0, header, 0.0)
    return own, before.astype(BF), header.astype(BF)


def returned(before, header):
    return [
        lax.ppermute(before, "y", turned(4, 3)),
        lax.ppermute(header, "y", turned(4, 2)),
        lax.ppermute(header, "y", turned(4, 1)),
    ]


def summed(own, got, y):
    from_next, third, last = (value.astype(F32) for value in got)
    return (own + from_next + jnp.where(y == 0, third + last, 0.0)).astype(BF)


def on_device(hidden_in, queries, saved_keys, value_matrix, output_gradient, passage_index):
    y, zh, zl = lax.axis_index("y"), lax.axis_index("zh"), lax.axis_index("zl")
    x, c = lax.axis_index("x"), lax.axis_index("c")
    z, s = lax.axis_index(("zh", "zl")), lax.axis_index(SEQ)
    hidden, q, k, g = hidden_in[0], queries[0], saved_keys[0], output_gradient[0]
    width, kv = hidden.shape[1], k.shape[1]
    each, half = width // 16, width // 2
    two = 2 * each

    k_before, k_header, k_sent = nearby(k, y, zh)
    k_other = lax.ppermute(k_sent, "zh", SWAP)
    k_slots = placed(k, k_before, k_header, k_other, zh)

    by_x = jnp.stack(
        [
            jnp.concatenate(
                [hidden[:, i * two : (i + 1) * two], hidden[:, half + i * two : half + (i + 1) * two]],
                axis=1,
            )
            for i in range(4)
        ]
    )
    crossed = lax.all_to_all(after(by_x, k_sent), "x", 0, 0).reshape(4 * ROWS, 4 * each)
    across = lax.ppermute(value_matrix, "zl", SWAP)
    planes = jnp.where(
        zl == 0, jnp.stack([value_matrix, across]), jnp.stack([across, value_matrix])
    )
    sibling = lax.ppermute(planes, "c", SWAP)
    weight = jnp.where(
        c == 0, jnp.stack([planes, sibling], 1), jnp.stack([sibling, planes], 1)
    ).reshape(4 * each, kv)

    bias = slot_bias(passage_index[0], s)
    probs, dv_slots = probs_call(q, k_slots, g, bias)
    dv_header, dv_sent = parted(dv_slots, zh)
    dv_sent = after(dv_sent, crossed)
    dv_other = lax.ppermute(dv_sent, "zh", SWAP)

    part = jnp.dot(
        after(crossed, dv_sent), weight, preferred_element_type=F32
    ).reshape(4, ROWS, kv)
    values = block_at(part, x)
    sends = [block_at(part, (x + step) % 4).astype(BF) for step in (1, 2, 3)]
    v_terms = [
        lax.ppermute(sent, "x", turned(4, step)) for step, sent in zip((1, 2, 3), sends)
    ]

    (dv_other,) = held([dv_other], sends)
    dv_own, dv_before, dv_header = joined(dv_slots, dv_header, dv_other, y, zh)
    dv_got = returned(dv_before, dv_header)

    for term in held(v_terms, [dv_before, dv_header]):
        values = values + term.astype(F32)
    values = values.astype(BF)
    v_before, v_header, v_sent = nearby(values, y, zh)

    value_grad = summed(dv_own, held(dv_got, [values]), y)
    near = turns(value_grad, "x", 4)
    v_sent = after(v_sent, value_grad)
    v_other = lax.ppermute(v_sent, "zh", SWAP)

    near = [value_grad] + list(held(near, [v_sent]))
    back, kept, given = grads_call(jnp.stack([x, c]), crossed, weight, near)
    sibling_term = lax.ppermute(given, "c", SWAP)
    quarters_of = (2, 2, each // 2, kv)
    kept, sibling_term = kept.reshape(quarters_of), sibling_term.reshape(quarters_of)

    def quarter(at):
        where = (at % 2, at // 2, 0, 0)
        block = (1, 1, each // 2, kv)
        mine, theirs = (lax.dynamic_slice(t, where, block)[0, 0] for t in (kept, sibling_term))
        return mine + theirs.astype(F32)

    total = quarter(z)
    quarters = [quarter((z + step) % 4).astype(BF) for step in (1, 2, 3)]
    z_terms = [
        lax.ppermute(sent, ("zh", "zl"), turned(4, step))
        for step, sent in zip((1, 2, 3), quarters)
    ]

    (v_other,) = held([v_other], quarters)
    v_slots = placed(values, v_before, v_header, v_other, zh)
    dq, dk_slots = scores_call(q, k_slots, g, v_slots, probs)

    for term in z_terms:
        total = total + term.astype(F32)
    mine = total.astype(BF)
    dk_header, dk_sent = parted(dk_slots, zh)
    dk_other = lax.ppermute(dk_sent, "zh", SWAP)

    terms = turns(mine, "y", 4)
    first, second, third = (term.astype(F32) for term in terms)
    total = ((mine.astype(F32) + second) + (first + third)).astype(BF)
    other = lax.ppermute(total, "zh", SWAP)

    dk_own, dk_before, dk_header = joined(dk_slots, dk_header, dk_other, y, zh)
    dk_got = returned(dk_before, dk_header)
    (other,) = held([other], [dk_before, dk_header])
    grad_weight = jnp.where(
        zh == 0, jnp.concatenate([total, other]), jnp.concatenate([other, total])
    ).astype(F32)

    back = lax.all_to_all(back.reshape(4, ROWS, 4 * each), "x", 0, 0)
    grad_input = jnp.concatenate(
        [back[i][:, p * two : (p + 1) * two] for p in range(2) for i in range(4)], axis=1
    )

    key_grad = summed(dk_own, dk_got, y)
    return dq[None], key_grad[None], grad_input[None], grad_weight


def solution(mesh):
    fine = Mesh(mesh.devices.reshape(4, 2, 2, 4, 2), ("y", "zh", "zl", "x", "c"))
    tokens = P(FSDP, SEQ, None)
    return jax.shard_map(
        on_device,
        mesh=fine,
        in_specs=(tokens, tokens, tokens, P(FSDP, None), tokens, P(FSDP, None)),
        out_specs=(tokens, tokens, tokens, P(FSDP, None)),
        check_vma=False,
    )
```

```python
import math

import jax
import jax.numpy as jnp
from jax import lax
from jax.experimental import pallas as pl
from jax.experimental.pallas import tpu as pltpu
from jax.sharding import Mesh
from jax.sharding import PartitionSpec as P

KEY_HEADS = 4
GROUP = 8
HEAD = 128
ROWS = 128
BACK = 192
SLOTS = 2 * BACK + ROWS
SEQ = ("y", "zh")
FSDP = ("zl", "x", "c")
SWAP = ((0, 1), (1, 0))
ROOT = 1.0 / math.sqrt(HEAD)
BF = jnp.bfloat16
F32 = jnp.float32


def stacked(ref):
    return jnp.concatenate([ref[:, h * HEAD : (h + 1) * HEAD] for h in range(GROUP)], axis=0)


def probs_kernel(q_ref, k_ref, g_ref, bias_ref, p_ref, dv_ref):
    scores = lax.dot_general(
        k_ref[...], stacked(q_ref), (((1,), (1,)), ((), ())), preferred_element_type=F32
    )
    bias = bias_ref[...]
    scores = scores + jnp.concatenate([bias] * GROUP, axis=1)
    highest = jnp.max(scores, axis=0, keepdims=True)
    weights = jnp.exp((scores - highest) * ROOT)
    total = jnp.sum(weights, axis=0, keepdims=True)
    probs = (weights * (1.0 / total)).astype(BF)
    p_ref[0] = probs
    dv_ref[...] = jnp.dot(probs, stacked(g_ref), preferred_element_type=F32)


def scores_kernel(q_ref, k_ref, g_ref, v_ref, p_ref, dq_ref, dk_ref):
    dprobs = lax.dot_general(
        v_ref[...], stacked(g_ref), (((1,), (1,)), ((), ())), preferred_element_type=F32
    )
    probs = p_ref[0].astype(F32)
    delta = jnp.sum(probs * dprobs, axis=0, keepdims=True)
    dscores = (probs * (dprobs - delta) * ROOT).astype(BF)
    dk_ref[...] = jnp.dot(dscores, stacked(q_ref), preferred_element_type=F32)
    dq = lax.dot_general(
        k_ref[...], dscores, (((0,), (0,)), ((), ())), preferred_element_type=F32
    )
    for h in range(GROUP):
        part = slice(h * HEAD, (h + 1) * HEAD)
        dq_ref[:, part] = dq[:, part].T.astype(BF)


def far(value):
    return pltpu.with_memory_space_constraint(value, pltpu.HBM)


def column(rows, width):
    return pl.BlockSpec((rows, width), lambda g: (0, g))


def probs_call(q, k, g, bias):
    return pl.pallas_call(
        probs_kernel,
        grid=(KEY_HEADS,),
        in_specs=[
            column(ROWS, GROUP * HEAD),
            column(SLOTS, HEAD),
            column(ROWS, GROUP * HEAD),
            pl.BlockSpec((SLOTS, ROWS), lambda g: (0, 0)),
        ],
        out_specs=[
            pl.BlockSpec((1, SLOTS, GROUP * ROWS), lambda g: (g, 0, 0)),
            column(SLOTS, HEAD),
        ],
        out_shape=[
            pltpu.HBM((KEY_HEADS, SLOTS, GROUP * ROWS), BF),
            jax.ShapeDtypeStruct((SLOTS, KEY_HEADS * HEAD), F32),
        ],
        compiler_params=pltpu.CompilerParams(vmem_limit_bytes=24 << 20),
        cost_estimate=pl.CostEstimate(
            flops=SLOTS * ROWS, bytes_accessed=SLOTS * ROWS, transcendentals=0
        ),
        name="probs",
    )(q, k, g, bias)


def scores_call(q, k, g, v, p):
    return pl.pallas_call(
        scores_kernel,
        grid=(KEY_HEADS,),
        in_specs=[
            column(ROWS, GROUP * HEAD),
            column(SLOTS, HEAD),
            column(ROWS, GROUP * HEAD),
            column(SLOTS, HEAD),
            pl.BlockSpec((1, SLOTS, GROUP * ROWS), lambda g: (g, 0, 0)),
        ],
        out_specs=[column(ROWS, GROUP * HEAD), column(SLOTS, HEAD)],
        out_shape=[
            jax.ShapeDtypeStruct((ROWS, KEY_HEADS * GROUP * HEAD), BF),
            jax.ShapeDtypeStruct((SLOTS, KEY_HEADS * HEAD), F32),
        ],
        compiler_params=pltpu.CompilerParams(vmem_limit_bytes=24 << 20),
        cost_estimate=pl.CostEstimate(
            flops=6 * SLOTS * ROWS * 32 * HEAD, bytes_accessed=8 << 20, transcendentals=0
        ),
        name="scores",
    )(far(q), k, far(g), v, far(p))


def slot_bias(passages, s):
    token = s * ROWS + jnp.arange(ROWS)
    mine = lax.dynamic_slice(passages, (s * ROWS,), (ROWS,))
    padded = jnp.concatenate([jnp.zeros((BACK,), passages.dtype), passages])
    near = lax.dynamic_slice(padded, (s * ROWS,), (BACK + ROWS,))
    head_ok = (passages[:BACK, None] == 0) & (jnp.arange(BACK)[:, None] <= token[None])
    near_token = s * ROWS - BACK + jnp.arange(BACK + ROWS)
    near_ok = (
        (near[:, None] == mine[None])
        & (near[:, None] != 0)
        & (near_token[:, None] <= token[None])
    )
    return jnp.where(jnp.concatenate([head_ok, near_ok]), 0.0, -1e30).astype(F32)


def grads_kernel(at_ref, crossed_ref, weight_ref, *refs):
    nears, (back_ref, kept_ref, given_ref, gathered_ref) = refs[:4], refs[4:]
    x, c = at_ref[0], at_ref[1]
    for n in range(4):
        row = pl.multiple_of((x + 4 - n) % 4 * ROWS, ROWS)
        gathered_ref[pl.ds(row, ROWS), :] = nears[n][...]
    gathered = gathered_ref[...]
    term = lax.dot_general(
        crossed_ref[...], gathered, (((0,), (0,)), ((), ())), preferred_element_type=F32
    )
    each = term.shape[0] // 2
    kept_ref[0] = jnp.where(c == 0, term[:each], term[each:])
    given_ref[0] = jnp.where(c == 0, term[each:], term[:each]).astype(BF)
    back_ref[...] = lax.dot_general(
        gathered, weight_ref[...], (((1,), (1,)), ((), ())), preferred_element_type=F32
    ).astype(BF)


def grads_call(at, crossed, weight, nears):
    rows, columns = crossed.shape
    kv, half, each = weight.shape[1], columns // 2, columns // 4
    piece = pl.BlockSpec((1, each, kv), lambda i, at: (i, 0, 0))
    return pl.pallas_call(
        grads_kernel,
        grid_spec=pltpu.PrefetchScalarGridSpec(
            num_scalar_prefetch=1,
            grid=(2,),
            in_specs=[
                pl.BlockSpec((rows, half), lambda i, at: (0, i)),
                pl.BlockSpec((half, kv), lambda i, at: (i, 0)),
            ]
            + [pl.BlockSpec((ROWS, kv), lambda i, at: (0, 0))] * 4,
            out_specs=[pl.BlockSpec((rows, half), lambda i, at: (0, i)), piece, piece],
            scratch_shapes=[pltpu.VMEM((rows, kv), BF)],
        ),
        out_shape=[
            pltpu.HBM((rows, columns), BF),
            pltpu.HBM((2, each, kv), F32),
            jax.ShapeDtypeStruct((2, each, kv), BF),
        ],
        compiler_params=pltpu.CompilerParams(vmem_limit_bytes=24 << 20),
        cost_estimate=pl.CostEstimate(
            flops=4 * rows * columns * kv, bytes_accessed=8 << 20, transcendentals=0
        ),
        name="grads",
    )(at, crossed, weight, *nears)


def turned(count, step):
    return tuple((i, (i + step) % count) for i in range(count))


def block_at(array, index):
    return lax.dynamic_index_in_dim(array, index, 0, keepdims=False)


def after(value, *others):
    return lax.optimization_barrier((value,) + others)[0]


def held(values, others):
    return lax.optimization_barrier((tuple(values), tuple(others)))[0]


def turns(value, axis, count, steps=(1, 2, 3)):
    return [lax.ppermute(value, axis, turned(count, n)) for n in steps]


def nearby(block, y, zh):
    before, third, last = turns(block, "y", 4)
    header = jnp.where(
        y == 0, block, jnp.where(y == 1, before, jnp.where(y == 2, third, last))
    )
    return before, header, jnp.concatenate([jnp.where(zh == 0, block, before), header])


def placed(block, before, header, other, zh):
    tail = 2 * ROWS - BACK
    nearest, header_too = other[:ROWS], other[ROWS:]
    low = jnp.where(zh == 0, header, header_too)
    high = jnp.where(zh == 0, header_too, header)
    return jnp.concatenate([low, high[:tail], before[tail:], nearest, block])


def parted(slots, zh):
    low = slots[:ROWS]
    high = jnp.concatenate([slots[ROWS:BACK], jnp.zeros_like(slots[BACK:2 * ROWS])])
    nearest = slots[2 * BACK - ROWS : 2 * BACK]
    sent = jnp.concatenate([nearest, jnp.where(zh == 0, high, low)]).astype(BF)
    return jnp.where(zh == 0, low, high), sent


def joined(slots, header, other, y, zh):
    nearest, header_too = other[:ROWS].astype(F32), other[ROWS:].astype(F32)
    header = header + header_too
    tail = slots[BACK : 2 * BACK - ROWS]
    before = jnp.concatenate([jnp.zeros_like(tail), tail])
    before = before + jnp.where(zh == 1, nearest, 0.0) + jnp.where(y == 1, header, 0.0)
    own = slots[2 * BACK :] + jnp.where(zh == 0, nearest, 0.0) + jnp.where(y == 0, header, 0.0)
    return own, before.astype(BF), header.astype(BF)


def returned(before, header):
    return [
        lax.ppermute(before, "y", turned(4, 3)),
        lax.ppermute(header, "y", turned(4, 2)),
        lax.ppermute(header, "y", turned(4, 1)),
    ]


def summed(own, got, y):
    from_next, third, last = (value.astype(F32) for value in got)
    return (own + from_next + jnp.where(y == 0, third + last, 0.0)).astype(BF)


def on_device(hidden_in, queries, saved_keys, value_matrix, output_gradient, passage_index):
    y, zh, zl = lax.axis_index("y"), lax.axis_index("zh"), lax.axis_index("zl")
    x, c = lax.axis_index("x"), lax.axis_index("c")
    z, s = lax.axis_index(("zh", "zl")), lax.axis_index(SEQ)
    hidden, q, k, g = hidden_in[0], queries[0], saved_keys[0], output_gradient[0]
    width, kv = hidden.shape[1], k.shape[1]
    each, half = width // 16, width // 2
    two = 2 * each

    k_before, k_header, k_sent = nearby(k, y, zh)
    k_other = lax.ppermute(k_sent, "zh", SWAP)
    k_slots = placed(k, k_before, k_header, k_other, zh)

    by_x = jnp.stack(
        [
            jnp.concatenate(
                [hidden[:, i * two : (i + 1) * two], hidden[:, half + i * two : half + (i + 1) * two]],
                axis=1,
            )
            for i in range(4)
        ]
    )
    crossed = lax.all_to_all(after(by_x, k_sent), "x", 0, 0).reshape(4 * ROWS, 4 * each)
    across = lax.ppermute(value_matrix, "zl", SWAP)
    planes = jnp.where(
        zl == 0, jnp.stack([value_matrix, across]), jnp.stack([across, value_matrix])
    )
    sibling = lax.ppermute(planes, "c", SWAP)
    weight = jnp.where(
        c == 0, jnp.stack([planes, sibling], 1), jnp.stack([sibling, planes], 1)
    ).reshape(4 * each, kv)

    bias = slot_bias(after(passage_index, k_sent)[0], s)
    probs, dv_slots = probs_call(q, k_slots, g, bias)
    dv_header, dv_sent = parted(dv_slots, zh)
    dv_other = lax.ppermute(dv_sent, "zh", SWAP)

    part = jnp.dot(
        after(crossed, dv_sent), weight, preferred_element_type=F32
    ).reshape(4, ROWS, kv)
    values = block_at(part, x)
    sends = [block_at(part, (x + step) % 4).astype(BF) for step in (1, 2, 3)]
    v_terms = [
        lax.ppermute(sent, "x", turned(4, step)) for step, sent in zip((1, 2, 3), sends)
    ]

    (dv_other,) = held([dv_other], sends)
    dv_own, dv_before, dv_header = joined(dv_slots, dv_header, dv_other, y, zh)
    dv_got = returned(dv_before, dv_header)

    for term in held(v_terms, [dv_before, dv_header]):
        values = values + term.astype(F32)
    values = values.astype(BF)
    v_before, v_header, v_sent = nearby(values, y, zh)

    value_grad = summed(dv_own, held(dv_got, [values]), y)
    near = turns(value_grad, "x", 4)
    v_sent = after(v_sent, value_grad)
    v_other = lax.ppermute(v_sent, "zh", SWAP)

    near = [value_grad] + list(held(near, [v_sent]))
    back, kept, given = grads_call(jnp.stack([x, c]), crossed, weight, near)
    sibling_term = lax.ppermute(given, "c", SWAP)
    quarters_of = (2, 2, each // 2, kv)
    kept, sibling_term = kept.reshape(quarters_of), sibling_term.reshape(quarters_of)

    def quarter(at):
        where = (at % 2, at // 2, 0, 0)
        block = (1, 1, each // 2, kv)
        mine, theirs = (lax.dynamic_slice(t, where, block)[0, 0] for t in (kept, sibling_term))
        return mine + theirs.astype(F32)

    total = quarter(z)
    quarters = [quarter((z + step) % 4).astype(BF) for step in (1, 2, 3)]
    z_terms = [
        lax.ppermute(sent, ("zh", "zl"), turned(4, step))
        for step, sent in zip((1, 2, 3), quarters)
    ]

    (v_other,) = held([v_other], quarters)
    v_slots = placed(values, v_before, v_header, v_other, zh)
    dq, dk_slots = scores_call(q, k_slots, g, v_slots, probs)

    for term in z_terms:
        total = total + term.astype(F32)
    mine = total.astype(BF)
    dk_header, dk_sent = parted(dk_slots, zh)
    dk_other = lax.ppermute(dk_sent, "zh", SWAP)

    terms = turns(mine, "y", 4)
    first, second, third = (term.astype(F32) for term in terms)
    total = ((mine.astype(F32) + second) + (first + third)).astype(BF)
    other = lax.ppermute(total, "zh", SWAP)

    dk_own, dk_before, dk_header = joined(dk_slots, dk_header, dk_other, y, zh)
    dk_got = returned(dk_before, dk_header)
    (other,) = held([other], [dk_before, dk_header])
    grad_weight = jnp.where(
        zh == 0, jnp.concatenate([total, other]), jnp.concatenate([other, total])
    ).astype(F32)

    back = lax.all_to_all(back.reshape(4, ROWS, 4 * each), "x", 0, 0)
    (back,) = held([back], [dk_before, dk_header, total])
    grad_input = jnp.concatenate(
        [back[i][:, p * two : (p + 1) * two] for p in range(2) for i in range(4)], axis=1
    )

    key_grad = summed(dk_own, dk_got, y)
    return dq[None], key_grad[None], grad_input[None], grad_weight


def solution(mesh):
    fine = Mesh(mesh.devices.reshape(4, 2, 2, 4, 2), ("y", "zh", "zl", "x", "c"))
    tokens = P(FSDP, SEQ, None)
    return jax.shard_map(
        on_device,
        mesh=fine,
        in_specs=(tokens, tokens, tokens, P(FSDP, None), tokens, P(FSDP, None)),
        out_specs=(tokens, tokens, tokens, P(FSDP, None)),
        check_vma=False,
    )
```

```python
import math

import jax
import jax.numpy as jnp
from jax import lax
from jax.experimental import pallas as pl
from jax.experimental.pallas import tpu as pltpu
from jax.sharding import Mesh
from jax.sharding import PartitionSpec as P

KEY_HEADS = 4
GROUP = 8
HEAD = 128
ROWS = 128
BACK = 192
SLOTS = 2 * BACK + ROWS
SEQ = ("y", "zh")
FSDP = ("zl", "x", "c")
SWAP = ((0, 1), (1, 0))
ROOT = 1.0 / math.sqrt(HEAD)
BF = jnp.bfloat16
F32 = jnp.float32


def stacked(ref):
    return jnp.concatenate([ref[:, h * HEAD : (h + 1) * HEAD] for h in range(GROUP)], axis=0)


def probs_kernel(q_ref, k_ref, g_ref, bias_ref, p_ref, dv_ref):
    scores = lax.dot_general(
        k_ref[...], stacked(q_ref), (((1,), (1,)), ((), ())), preferred_element_type=F32
    )
    bias = bias_ref[...]
    scores = scores + jnp.concatenate([bias] * GROUP, axis=1)
    highest = jnp.max(scores, axis=0, keepdims=True)
    weights = jnp.exp2((scores - highest) * (ROOT * math.log2(math.e)))
    total = jnp.sum(weights, axis=0, keepdims=True)
    probs = (weights * (1.0 / total)).astype(BF)
    p_ref[0] = probs
    dv_ref[...] = jnp.dot(probs, stacked(g_ref), preferred_element_type=F32)


def scores_kernel(q_ref, k_ref, g_ref, v_ref, p_ref, dq_ref, dk_ref):
    dprobs = lax.dot_general(
        v_ref[...], stacked(g_ref), (((1,), (1,)), ((), ())), preferred_element_type=F32
    )
    probs = p_ref[0].astype(F32)
    delta = jnp.sum(probs * dprobs, axis=0, keepdims=True)
    dscores = (probs * (dprobs - delta) * ROOT).astype(BF)
    dk_ref[...] = jnp.dot(dscores, stacked(q_ref), preferred_element_type=F32)
    dq = lax.dot_general(
        k_ref[...], dscores, (((0,), (0,)), ((), ())), preferred_element_type=F32
    )
    for h in range(GROUP):
        part = slice(h * HEAD, (h + 1) * HEAD)
        dq_ref[:, part] = dq[:, part].T.astype(BF)


def far(value):
    return pltpu.with_memory_space_constraint(value, pltpu.HBM)


def column(rows, width):
    return pl.BlockSpec((rows, width), lambda g: (0, g))


def probs_call(q, k, g, bias):
    return pl.pallas_call(
        probs_kernel,
        grid=(KEY_HEADS,),
        in_specs=[
            column(ROWS, GROUP * HEAD),
            column(SLOTS, HEAD),
            column(ROWS, GROUP * HEAD),
            pl.BlockSpec((SLOTS, ROWS), lambda g: (0, 0)),
        ],
        out_specs=[
            pl.BlockSpec((1, SLOTS, GROUP * ROWS), lambda g: (g, 0, 0)),
            column(SLOTS, HEAD),
        ],
        out_shape=[
            pltpu.HBM((KEY_HEADS, SLOTS, GROUP * ROWS), BF),
            jax.ShapeDtypeStruct((SLOTS, KEY_HEADS * HEAD), F32),
        ],
        compiler_params=pltpu.CompilerParams(vmem_limit_bytes=24 << 20),
        cost_estimate=pl.CostEstimate(
            flops=SLOTS * ROWS, bytes_accessed=SLOTS * ROWS, transcendentals=0
        ),
        name="probs",
    )(q, k, g, bias)


def scores_call(q, k, g, v, p):
    return pl.pallas_call(
        scores_kernel,
        grid=(KEY_HEADS,),
        in_specs=[
            column(ROWS, GROUP * HEAD),
            column(SLOTS, HEAD),
            column(ROWS, GROUP * HEAD),
            column(SLOTS, HEAD),
            pl.BlockSpec((1, SLOTS, GROUP * ROWS), lambda g: (g, 0, 0)),
        ],
        out_specs=[column(ROWS, GROUP * HEAD), column(SLOTS, HEAD)],
        out_shape=[
            jax.ShapeDtypeStruct((ROWS, KEY_HEADS * GROUP * HEAD), BF),
            jax.ShapeDtypeStruct((SLOTS, KEY_HEADS * HEAD), F32),
        ],
        compiler_params=pltpu.CompilerParams(vmem_limit_bytes=24 << 20),
        cost_estimate=pl.CostEstimate(
            flops=6 * SLOTS * ROWS * 32 * HEAD, bytes_accessed=8 << 20, transcendentals=0
        ),
        name="scores",
    )(far(q), k, far(g), v, far(p))


def slot_bias(passages, s):
    token = s * ROWS + jnp.arange(ROWS)
    mine = lax.dynamic_slice(passages, (s * ROWS,), (ROWS,))
    padded = jnp.concatenate([jnp.zeros((BACK,), passages.dtype), passages])
    near = lax.dynamic_slice(padded, (s * ROWS,), (BACK + ROWS,))
    head_ok = (passages[:BACK, None] == 0) & (jnp.arange(BACK)[:, None] <= token[None])
    near_token = s * ROWS - BACK + jnp.arange(BACK + ROWS)
    near_ok = (
        (near[:, None] == mine[None])
        & (near[:, None] != 0)
        & (near_token[:, None] <= token[None])
    )
    return jnp.where(jnp.concatenate([head_ok, near_ok]), 0.0, -1e30).astype(F32)


def grads_kernel(at_ref, crossed_ref, weight_ref, *refs):
    nears, (back_ref, kept_ref, given_ref, gathered_ref) = refs[:4], refs[4:]
    x, c = at_ref[0], at_ref[1]
    for n in range(4):
        row = pl.multiple_of((x + 4 - n) % 4 * ROWS, ROWS)
        gathered_ref[pl.ds(row, ROWS), :] = nears[n][...]
    gathered = gathered_ref[...]
    term = lax.dot_general(
        crossed_ref[...], gathered, (((0,), (0,)), ((), ())), preferred_element_type=F32
    )
    each = term.shape[0] // 2
    kept_ref[0] = jnp.where(c == 0, term[:each], term[each:])
    given_ref[0] = jnp.where(c == 0, term[each:], term[:each]).astype(BF)
    back_ref[...] = lax.dot_general(
        gathered, weight_ref[...], (((1,), (1,)), ((), ())), preferred_element_type=F32
    ).astype(BF)


def grads_call(at, crossed, weight, nears):
    rows, columns = crossed.shape
    kv, half, each = weight.shape[1], columns // 2, columns // 4
    piece = pl.BlockSpec((1, each, kv), lambda i, at: (i, 0, 0))
    return pl.pallas_call(
        grads_kernel,
        grid_spec=pltpu.PrefetchScalarGridSpec(
            num_scalar_prefetch=1,
            grid=(2,),
            in_specs=[
                pl.BlockSpec((rows, half), lambda i, at: (0, i)),
                pl.BlockSpec((half, kv), lambda i, at: (i, 0)),
            ]
            + [pl.BlockSpec((ROWS, kv), lambda i, at: (0, 0))] * 4,
            out_specs=[pl.BlockSpec((rows, half), lambda i, at: (0, i)), piece, piece],
            scratch_shapes=[pltpu.VMEM((rows, kv), BF)],
        ),
        out_shape=[
            pltpu.HBM((rows, columns), BF),
            pltpu.HBM((2, each, kv), F32),
            jax.ShapeDtypeStruct((2, each, kv), BF),
        ],
        compiler_params=pltpu.CompilerParams(vmem_limit_bytes=24 << 20),
        cost_estimate=pl.CostEstimate(
            flops=4 * rows * columns * kv, bytes_accessed=8 << 20, transcendentals=0
        ),
        name="grads",
    )(at, crossed, weight, *nears)


def turned(count, step):
    return tuple((i, (i + step) % count) for i in range(count))


def block_at(array, index):
    return lax.dynamic_index_in_dim(array, index, 0, keepdims=False)


def after(value, *others):
    return lax.optimization_barrier((value,) + others)[0]


def held(values, others):
    return lax.optimization_barrier((tuple(values), tuple(others)))[0]


def turns(value, axis, count):
    first, last, second = (lax.ppermute(value, axis, turned(count, n)) for n in (1, 3, 2))
    return [first, second, last]


def nearby(block, y, zh):
    before, third, last = turns(block, "y", 4)
    header = jnp.where(
        y == 0, block, jnp.where(y == 1, before, jnp.where(y == 2, third, last))
    )
    return before, header, jnp.concatenate([jnp.where(zh == 0, block, before), header])


def placed(block, before, header, other, zh):
    tail = 2 * ROWS - BACK
    nearest, header_too = other[:ROWS], other[ROWS:]
    low = jnp.where(zh == 0, header, header_too)
    high = jnp.where(zh == 0, header_too, header)
    return jnp.concatenate([low, high[:tail], before[tail:], nearest, block])


def parted(slots, zh):
    low = slots[:ROWS]
    high = jnp.concatenate([slots[ROWS:BACK], jnp.zeros_like(slots[BACK:2 * ROWS])])
    nearest = slots[2 * BACK - ROWS : 2 * BACK]
    sent = jnp.concatenate([nearest, jnp.where(zh == 0, high, low)]).astype(BF)
    return jnp.where(zh == 0, low, high), sent


def joined(slots, header, other, y, zh):
    nearest, header_too = other[:ROWS].astype(F32), other[ROWS:].astype(F32)
    header = header + header_too
    tail = slots[BACK : 2 * BACK - ROWS]
    before = jnp.concatenate([jnp.zeros_like(tail), tail])
    before = before + jnp.where(zh == 1, nearest, 0.0) + jnp.where(y == 1, header, 0.0)
    own = slots[2 * BACK :] + jnp.where(zh == 0, nearest, 0.0) + jnp.where(y == 0, header, 0.0)
    return own, before.astype(BF), header.astype(BF)


def returned(before, header):
    from_next = lax.ppermute(before, "y", turned(4, 3))
    last = lax.ppermute(header, "y", turned(4, 1))
    return [from_next, lax.ppermute(header, "y", turned(4, 2)), last]


def summed(own, got, y):
    from_next, third, last = (value.astype(F32) for value in got)
    return (own + from_next + jnp.where(y == 0, third + last, 0.0)).astype(BF)


def on_device(hidden_in, queries, saved_keys, value_matrix, output_gradient, passage_index):
    y, zh, zl = lax.axis_index("y"), lax.axis_index("zh"), lax.axis_index("zl")
    x, c = lax.axis_index("x"), lax.axis_index("c")
    z, s = lax.axis_index(("zh", "zl")), lax.axis_index(SEQ)
    hidden, q, k, g = hidden_in[0], queries[0], saved_keys[0], output_gradient[0]
    width, kv = hidden.shape[1], k.shape[1]
    each, half = width // 16, width // 2
    two = 2 * each

    k_before, k_header, k_sent = nearby(k, y, zh)
    k_other = lax.ppermute(k_sent, "zh", SWAP)
    k_slots = placed(k, k_before, k_header, k_other, zh)

    by_x = jnp.stack(
        [
            jnp.concatenate(
                [hidden[:, i * two : (i + 1) * two], hidden[:, half + i * two : half + (i + 1) * two]],
                axis=1,
            )
            for i in range(4)
        ]
    )
    crossed = lax.all_to_all(after(by_x, k_sent), "x", 0, 0).reshape(4 * ROWS, 4 * each)
    across = lax.ppermute(value_matrix, "zl", SWAP)
    planes = jnp.where(
        zl == 0, jnp.stack([value_matrix, across]), jnp.stack([across, value_matrix])
    )
    sibling = lax.ppermute(planes, "c", SWAP)
    weight = jnp.where(
        c == 0, jnp.stack([planes, sibling], 1), jnp.stack([sibling, planes], 1)
    ).reshape(4 * each, kv)

    bias = slot_bias(after(passage_index, k_sent)[0], s)
    probs, dv_slots = probs_call(q, k_slots, g, bias)
    dv_header, dv_sent = parted(dv_slots, zh)
    dv_other = lax.ppermute(dv_sent, "zh", SWAP)

    part = jnp.dot(
        after(crossed, dv_sent), weight, preferred_element_type=F32
    ).reshape(4, ROWS, kv)
    values = block_at(part, x)
    sends = [block_at(part, (x + step) % 4).astype(BF) for step in (1, 2, 3)]
    v_terms = [
        lax.ppermute(sent, "x", turned(4, step)) for step, sent in zip((1, 2, 3), sends)
    ]

    (dv_other,) = held([dv_other], sends)
    dv_own, dv_before, dv_header = joined(dv_slots, dv_header, dv_other, y, zh)
    dv_got = returned(dv_before, dv_header)

    for term in held(v_terms, [dv_before, dv_header]):
        values = values + term.astype(F32)
    values = values.astype(BF)
    v_before, v_header, v_sent = nearby(values, y, zh)

    value_grad = summed(dv_own, held(dv_got, [values]), y)
    near = turns(value_grad, "x", 4)
    v_sent = after(v_sent, value_grad)
    v_other = lax.ppermute(v_sent, "zh", SWAP)

    near = [value_grad] + list(held(near, [v_sent]))
    back, kept, given = grads_call(jnp.stack([x, c]), crossed, weight, near)
    sibling_term = lax.ppermute(given, "c", SWAP)
    quarters_of = (2, 2, each // 2, kv)
    kept, sibling_term = kept.reshape(quarters_of), sibling_term.reshape(quarters_of)

    def quarter(at):
        where = (at % 2, at // 2, 0, 0)
        block = (1, 1, each // 2, kv)
        mine, theirs = (lax.dynamic_slice(t, where, block)[0, 0] for t in (kept, sibling_term))
        return mine + theirs.astype(F32)

    total = quarter(z)
    quarters = [quarter((z + step) % 4).astype(BF) for step in (1, 2, 3)]
    z_terms = [
        lax.ppermute(sent, ("zh", "zl"), turned(4, step))
        for step, sent in zip((1, 2, 3), quarters)
    ]

    (v_other,) = held([v_other], quarters)
    v_slots = placed(values, v_before, v_header, v_other, zh)
    dq, dk_slots = scores_call(q, k_slots, g, v_slots, probs)

    for term in z_terms:
        total = total + term.astype(F32)
    mine = total.astype(BF)
    dk_header, dk_sent = parted(dk_slots, zh)
    dk_other = lax.ppermute(dk_sent, "zh", SWAP)

    terms = turns(mine, "y", 4)
    first, second, third = (term.astype(F32) for term in terms)
    total = ((mine.astype(F32) + second) + (first + third)).astype(BF)
    other = lax.ppermute(total, "zh", SWAP)

    dk_own, dk_before, dk_header = joined(dk_slots, dk_header, dk_other, y, zh)
    dk_got = returned(dk_before, dk_header)
    (other,) = held([other], [dk_before, dk_header])
    grad_weight = jnp.where(
        zh == 0, jnp.concatenate([total, other]), jnp.concatenate([other, total])
    ).astype(F32)

    back = lax.all_to_all(back.reshape(4, ROWS, 4 * each), "x", 0, 0)
    (back,) = held([back], [dk_before, dk_header, total])
    grad_input = jnp.concatenate(
        [back[i][:, p * two : (p + 1) * two] for p in range(2) for i in range(4)], axis=1
    )

    key_grad = summed(dk_own, dk_got, y)
    return dq[None], key_grad[None], grad_input[None], grad_weight


def solution(mesh):
    fine = Mesh(mesh.devices.reshape(4, 2, 2, 4, 2), ("y", "zh", "zl", "x", "c"))
    tokens = P(FSDP, SEQ, None)
    return jax.shard_map(
        on_device,
        mesh=fine,
        in_specs=(tokens, tokens, tokens, P(FSDP, None), tokens, P(FSDP, None)),
        out_specs=(tokens, tokens, tokens, P(FSDP, None)),
        check_vma=False,
    )
```

```python
import math

import jax
import jax.numpy as jnp
from jax import lax
from jax.experimental import pallas as pl
from jax.experimental.pallas import tpu as pltpu
from jax.sharding import Mesh
from jax.sharding import PartitionSpec as P

KEY_HEADS = 4
GROUP = 8
HEAD = 128
ROWS = 128
BACK = 192
SLOTS = 2 * BACK + ROWS
SEQ = ("y", "zh")
FSDP = ("zl", "x", "c")
SWAP = ((0, 1), (1, 0))
ROOT = 1.0 / math.sqrt(HEAD)
BF = jnp.bfloat16
F32 = jnp.float32


def stacked(ref):
    return jnp.concatenate([ref[:, h * HEAD : (h + 1) * HEAD] for h in range(GROUP)], axis=0)


def probs_kernel(q_ref, k_ref, g_ref, bias_ref, p_ref, dv_ref):
    scores = lax.dot_general(
        k_ref[...], stacked(q_ref), (((1,), (1,)), ((), ())), preferred_element_type=F32
    )
    bias = bias_ref[...]
    scores = scores + jnp.concatenate([bias] * GROUP, axis=1)
    highest = jnp.max(scores, axis=0, keepdims=True)
    weights = jnp.exp2((scores - highest) * (ROOT * math.log2(math.e)))
    total = jnp.sum(weights, axis=0, keepdims=True)
    probs = (weights * (1.0 / total)).astype(BF)
    p_ref[0] = probs
    dv_ref[...] = jnp.dot(probs, stacked(g_ref), preferred_element_type=F32)


def scores_kernel(q_ref, k_ref, g_ref, v_ref, p_ref, dq_ref, dk_ref):
    dprobs = lax.dot_general(
        v_ref[...], stacked(g_ref), (((1,), (1,)), ((), ())), preferred_element_type=F32
    )
    probs = p_ref[0].astype(F32)
    delta = jnp.sum(probs * dprobs, axis=0, keepdims=True)
    dscores = (probs * (dprobs - delta) * ROOT).astype(BF)
    dk_ref[...] = jnp.dot(dscores, stacked(q_ref), preferred_element_type=F32)
    dq = lax.dot_general(
        k_ref[...], dscores, (((0,), (0,)), ((), ())), preferred_element_type=F32
    )
    for h in range(GROUP):
        part = slice(h * HEAD, (h + 1) * HEAD)
        dq_ref[:, part] = dq[:, part].T.astype(BF)


def far(value):
    return pltpu.with_memory_space_constraint(value, pltpu.HBM)


def column(rows, width):
    return pl.BlockSpec((rows, width), lambda g: (0, g))


def probs_call(q, k, g, bias):
    return pl.pallas_call(
        probs_kernel,
        grid=(KEY_HEADS,),
        in_specs=[
            column(ROWS, GROUP * HEAD),
            column(SLOTS, HEAD),
            column(ROWS, GROUP * HEAD),
            pl.BlockSpec((SLOTS, ROWS), lambda g: (0, 0)),
        ],
        out_specs=[
            pl.BlockSpec((1, SLOTS, GROUP * ROWS), lambda g: (g, 0, 0)),
            column(SLOTS, HEAD),
        ],
        out_shape=[
            pltpu.HBM((KEY_HEADS, SLOTS, GROUP * ROWS), BF),
            jax.ShapeDtypeStruct((SLOTS, KEY_HEADS * HEAD), F32),
        ],
        compiler_params=pltpu.CompilerParams(vmem_limit_bytes=24 << 20),
        cost_estimate=pl.CostEstimate(
            flops=SLOTS * ROWS, bytes_accessed=SLOTS * ROWS, transcendentals=0
        ),
        name="probs",
    )(q, k, g, bias)


def scores_call(q, k, g, v, p):
    return pl.pallas_call(
        scores_kernel,
        grid=(KEY_HEADS,),
        in_specs=[
            column(ROWS, GROUP * HEAD),
            column(SLOTS, HEAD),
            column(ROWS, GROUP * HEAD),
            column(SLOTS, HEAD),
            pl.BlockSpec((1, SLOTS, GROUP * ROWS), lambda g: (g, 0, 0)),
        ],
        out_specs=[column(ROWS, GROUP * HEAD), column(SLOTS, HEAD)],
        out_shape=[
            jax.ShapeDtypeStruct((ROWS, KEY_HEADS * GROUP * HEAD), BF),
            jax.ShapeDtypeStruct((SLOTS, KEY_HEADS * HEAD), F32),
        ],
        compiler_params=pltpu.CompilerParams(vmem_limit_bytes=24 << 20),
        cost_estimate=pl.CostEstimate(
            flops=6 * SLOTS * ROWS * 32 * HEAD, bytes_accessed=8 << 20, transcendentals=0
        ),
        name="scores",
    )(far(q), k, far(g), v, far(p))


def slot_bias(passages, s):
    token = s * ROWS + jnp.arange(ROWS)
    mine = lax.dynamic_slice(passages, (s * ROWS,), (ROWS,))
    padded = jnp.concatenate([jnp.zeros((BACK,), passages.dtype), passages])
    near = lax.dynamic_slice(padded, (s * ROWS,), (BACK + ROWS,))
    head_ok = (passages[:BACK, None] == 0) & (jnp.arange(BACK)[:, None] <= token[None])
    near_token = s * ROWS - BACK + jnp.arange(BACK + ROWS)
    near_ok = (
        (near[:, None] == mine[None])
        & (near[:, None] != 0)
        & (near_token[:, None] <= token[None])
    )
    return jnp.where(jnp.concatenate([head_ok, near_ok]), 0.0, -1e30).astype(F32)


def grads_kernel(at_ref, crossed_ref, weight_ref, *refs):
    nears, (back_ref, kept_ref, given_ref, gathered_ref) = refs[:4], refs[4:]
    x, c = at_ref[0], at_ref[1]
    for n in range(4):
        row = pl.multiple_of((x + 4 - n) % 4 * ROWS, ROWS)
        gathered_ref[pl.ds(row, ROWS), :] = nears[n][...]
    gathered = gathered_ref[...]
    term = lax.dot_general(
        crossed_ref[...], gathered, (((0,), (0,)), ((), ())), preferred_element_type=F32
    )
    each = term.shape[0] // 2
    kept_ref[0] = jnp.where(c == 0, term[:each], term[each:])
    given_ref[0] = jnp.where(c == 0, term[each:], term[:each]).astype(BF)
    back_ref[...] = lax.dot_general(
        gathered, weight_ref[...], (((1,), (1,)), ((), ())), preferred_element_type=F32
    ).astype(BF)


def grads_call(at, crossed, weight, nears):
    rows, columns = crossed.shape
    kv, half, each = weight.shape[1], columns // 2, columns // 4
    piece = pl.BlockSpec((1, each, kv), lambda i, at: (i, 0, 0))
    return pl.pallas_call(
        grads_kernel,
        grid_spec=pltpu.PrefetchScalarGridSpec(
            num_scalar_prefetch=1,
            grid=(2,),
            in_specs=[
                pl.BlockSpec((rows, half), lambda i, at: (0, i)),
                pl.BlockSpec((half, kv), lambda i, at: (i, 0)),
            ]
            + [pl.BlockSpec((ROWS, kv), lambda i, at: (0, 0))] * 4,
            out_specs=[pl.BlockSpec((rows, half), lambda i, at: (0, i)), piece, piece],
            scratch_shapes=[pltpu.VMEM((rows, kv), BF)],
        ),
        out_shape=[
            pltpu.HBM((rows, columns), BF),
            pltpu.HBM((2, each, kv), F32),
            jax.ShapeDtypeStruct((2, each, kv), BF),
        ],
        compiler_params=pltpu.CompilerParams(vmem_limit_bytes=24 << 20),
        cost_estimate=pl.CostEstimate(
            flops=4 * rows * columns * kv, bytes_accessed=8 << 20, transcendentals=0
        ),
        name="grads",
    )(at, crossed, weight, *nears)


def turned(count, step):
    return tuple((i, (i + step) % count) for i in range(count))


def block_at(array, index):
    return lax.dynamic_index_in_dim(array, index, 0, keepdims=False)


def after(value, *others):
    return lax.optimization_barrier((value,) + others)[0]


def held(values, others):
    return lax.optimization_barrier((tuple(values), tuple(others)))[0]


def turns(value, axis, count):
    first, last, second = (lax.ppermute(value, axis, turned(count, n)) for n in (1, 3, 2))
    return [first, second, last]


def nearby(block, y, zh):
    before, third, last = turns(block, "y", 4)
    header = jnp.where(
        y == 0, block, jnp.where(y == 1, before, jnp.where(y == 2, third, last))
    )
    return before, header, jnp.concatenate([jnp.where(zh == 0, block, before), header])


def placed(block, before, header, other, zh):
    tail = 2 * ROWS - BACK
    nearest, header_too = other[:ROWS], other[ROWS:]
    low = jnp.where(zh == 0, header, header_too)
    high = jnp.where(zh == 0, header_too, header)
    return jnp.concatenate([low, high[:tail], before[tail:], nearest, block])


def parted(slots, zh):
    low = slots[:ROWS]
    high = jnp.concatenate([slots[ROWS:BACK], jnp.zeros_like(slots[BACK:2 * ROWS])])
    nearest = slots[2 * BACK - ROWS : 2 * BACK]
    sent = jnp.concatenate([nearest, jnp.where(zh == 0, high, low)]).astype(BF)
    return jnp.where(zh == 0, low, high), sent


def joined(slots, header, other, y, zh):
    nearest, header_too = other[:ROWS].astype(F32), other[ROWS:].astype(F32)
    header = header + header_too
    tail = slots[BACK : 2 * BACK - ROWS]
    before = jnp.concatenate([jnp.zeros_like(tail), tail])
    before = before + jnp.where(zh == 1, nearest, 0.0) + jnp.where(y == 1, header, 0.0)
    own = slots[2 * BACK :] + jnp.where(zh == 0, nearest, 0.0) + jnp.where(y == 0, header, 0.0)
    return own, before.astype(BF), header.astype(BF)


def returned(before, header):
    from_next = lax.ppermute(before, "y", turned(4, 3))
    last = lax.ppermute(header, "y", turned(4, 1))
    return [from_next, lax.ppermute(header, "y", turned(4, 2)), last]


def summed(own, got, y):
    from_next, third, last = (value.astype(F32) for value in got)
    return (own + from_next + jnp.where(y == 0, third + last, 0.0)).astype(BF)


def on_device(hidden_in, queries, saved_keys, value_matrix, output_gradient, passage_index):
    y, zh, zl = lax.axis_index("y"), lax.axis_index("zh"), lax.axis_index("zl")
    x, c = lax.axis_index("x"), lax.axis_index("c")
    z, s = lax.axis_index(("zh", "zl")), lax.axis_index(SEQ)
    hidden, q, k, g = hidden_in[0], queries[0], saved_keys[0], output_gradient[0]
    width, kv = hidden.shape[1], k.shape[1]
    each, half = width // 16, width // 2
    two = 2 * each

    k_before, k_header, k_sent = nearby(k, y, zh)
    k_other = lax.ppermute(k_sent, "zh", SWAP)
    k_slots = placed(k, k_before, k_header, k_other, zh)

    by_x = jnp.stack(
        [
            jnp.concatenate(
                [hidden[:, i * two : (i + 1) * two], hidden[:, half + i * two : half + (i + 1) * two]],
                axis=1,
            )
            for i in range(4)
        ]
    )
    crossed = lax.all_to_all(after(by_x, k_sent), "x", 0, 0).reshape(4 * ROWS, 4 * each)
    across = lax.ppermute(value_matrix, "zl", SWAP)
    planes = jnp.where(
        zl == 0, jnp.stack([value_matrix, across]), jnp.stack([across, value_matrix])
    )
    sibling = lax.ppermute(planes, "c", SWAP)
    weight = jnp.where(
        c == 0, jnp.stack([planes, sibling], 1), jnp.stack([sibling, planes], 1)
    ).reshape(4 * each, kv)

    bias = slot_bias(after(passage_index, k_sent)[0], s)
    probs, dv_slots = probs_call(q, k_slots, g, bias)
    dv_header, dv_sent = parted(dv_slots, zh)
    dv_other = lax.ppermute(dv_sent, "zh", SWAP)

    part = jnp.dot(
        after(crossed, dv_sent), weight, preferred_element_type=F32
    ).reshape(4, ROWS, kv)
    values = block_at(part, x)
    sends = [block_at(part, (x + step) % 4).astype(BF) for step in (1, 2, 3)]
    v_terms = [
        lax.ppermute(sent, "x", turned(4, step)) for step, sent in zip((1, 2, 3), sends)
    ]

    (dv_other,) = held([dv_other], sends)
    dv_own, dv_before, dv_header = joined(dv_slots, dv_header, dv_other, y, zh)
    dv_got = returned(dv_before, dv_header)

    for term in held(v_terms, [dv_before, dv_header]):
        values = values + term.astype(F32)
    values = values.astype(BF)
    v_before, v_header, v_sent = nearby(values, y, zh)

    value_grad = summed(dv_own, held(dv_got, [values]), y)
    near = turns(value_grad, "x", 4)
    v_other = lax.ppermute(v_sent, "zh", SWAP)

    near = [value_grad] + list(held(near, [v_sent]))
    back, kept, given = grads_call(jnp.stack([x, c]), crossed, weight, near)
    sibling_term = lax.ppermute(given, "c", SWAP)
    quarters_of = (2, 2, each // 2, kv)
    kept, sibling_term = kept.reshape(quarters_of), sibling_term.reshape(quarters_of)

    def quarter(at):
        where = (at % 2, at // 2, 0, 0)
        block = (1, 1, each // 2, kv)
        mine, theirs = (lax.dynamic_slice(t, where, block)[0, 0] for t in (kept, sibling_term))
        return mine + theirs.astype(F32)

    total = quarter(z)
    quarters = [quarter((z + step) % 4).astype(BF) for step in (1, 2, 3)]
    z_terms = [
        lax.ppermute(sent, ("zh", "zl"), turned(4, step))
        for step, sent in zip((1, 2, 3), quarters)
    ]

    (v_other,) = held([v_other], quarters)
    v_slots = placed(values, v_before, v_header, v_other, zh)
    dq, dk_slots = scores_call(q, k_slots, g, v_slots, probs)

    for term in z_terms:
        total = total + term.astype(F32)
    mine = total.astype(BF)
    dk_header, dk_sent = parted(dk_slots, zh)
    dk_other = lax.ppermute(dk_sent, "zh", SWAP)

    terms = turns(mine, "y", 4)
    first, second, third = (term.astype(F32) for term in terms)
    total = ((mine.astype(F32) + second) + (first + third)).astype(BF)
    other = lax.ppermute(total, "zh", SWAP)

    dk_own, dk_before, dk_header = joined(dk_slots, dk_header, dk_other, y, zh)
    dk_got = returned(dk_before, dk_header)
    (other,) = held([other], [dk_before, dk_header])
    grad_weight = jnp.where(
        zh == 0, jnp.concatenate([total, other]), jnp.concatenate([other, total])
    ).astype(F32)

    back = lax.all_to_all(back.reshape(4, ROWS, 4 * each), "x", 0, 0)
    (back,) = held([back], [dk_before, dk_header, total])
    grad_input = jnp.concatenate(
        [back[i][:, p * two : (p + 1) * two] for p in range(2) for i in range(4)], axis=1
    )

    key_grad = summed(dk_own, dk_got, y)
    return dq[None], key_grad[None], grad_input[None], grad_weight


def solution(mesh):
    fine = Mesh(mesh.devices.reshape(4, 2, 2, 4, 2), ("y", "zh", "zl", "x", "c"))
    tokens = P(FSDP, SEQ, None)
    return jax.shard_map(
        on_device,
        mesh=fine,
        in_specs=(tokens, tokens, tokens, P(FSDP, None), tokens, P(FSDP, None)),
        out_specs=(tokens, tokens, tokens, P(FSDP, None)),
        check_vma=False,
    )
```
